32 devices in a mesh: seg: 4 (over x, core), blk: 8 (over z, y).
Axes of the slice: x: 2, y: 2, z: 4, core: 2. Of those that a mesh axis runs over, the one named last changes fastest.
Arguments:
- start_state: float32 [32, 256, 256], P(('seg', 'blk')), may hold values from -6 to 6
- sector_sizes: int32 [32], P(('seg', 'blk')), may hold values from 128 to 256, as said below
- partner: int32 [32, 16], P(('seg', 'blk')), may hold values from 0 to 7
- left_diag: bfloat16 [32, 256, 256], P(('seg', 'blk')), may hold values from -2 to 4, as said below
- right_diag: bfloat16 [32, 256, 256], P(('seg', 'blk')), may hold values from -2 to 4, as said below
- left_hop: bfloat16 [32, 16, 256, 256], P(('seg', 'blk')), may hold values from -0.375 to 0.375
- right_hop: bfloat16 [32, 16, 256, 256], P(('seg', 'blk')), may hold values from -0.375 to 0.375
- left_coupling: float32 [4, 17], P('seg'), may hold values from 0.3 to 3
- right_coupling: float32 [4, 17], P('seg'), may hold values from 0.3 to 3
Outputs:
- state: float32 [32, 256, 256], P(('seg', 'blk'))
- energy: float32 [4], P('seg')
- left_boundary: bfloat16 [32, 256, 256], P(('seg', 'blk'))
- right_boundary: bfloat16 [32, 256, 256], P(('seg', 'blk'))
The draws below stay inside these ranges and needn't reach their ends.
Inputs may be any that keep to these rules, and one draw needn't show every extreme that they name: `sector_sizes`: in every segment one sector has exactly 256 live states and another exactly 128. `left_diag`: symmetric blocks with diagonal entries from 1 to 4. `right_diag`: symmetric blocks with diagonal entries from 1 to 4.
All inputs are finite; a program needn't handle non-finite values.
Results may differ from the reference program's by a relative error of at most 0.017.
Values may be sent and summed in bfloat16 or wider, within the bound.
A program may use at most 64 MiB of HBM per device.

```python
import math
import jax
import jax.numpy as jnp
from jax import lax

P_SIZE = 256
K = 16
ITERS = 4
Q = 8
SEGS = 4


def draw_sector_sizes(key, part):
    key = jax.random.fold_in(key, 1)
    first, second = jax.random.split(key)
    base = jax.random.randint(first, (SEGS, Q), P_SIZE // 2, P_SIZE + 1)
    order = jax.vmap(lambda sub: jax.random.permutation(sub, Q))(jax.random.split(second, SEGS))
    columns = jnp.arange(Q)[None, :]
    base = jnp.where(columns == order[:, 0:1], P_SIZE, base)
    base = jnp.where(columns == order[:, 1:2], P_SIZE // 2, base)
    return base.reshape(SEGS * Q).astype(jnp.int32)


def draw_left_diag(key, part):
    key = jax.random.fold_in(key, 2)
    first, second = jax.random.split(key)
    noise = jax.random.normal(first, (SEGS * Q, P_SIZE, P_SIZE), jnp.float32)
    diag = jax.random.uniform(second, (SEGS * Q, P_SIZE), jnp.float32, 1.0, 3.0)
    unit = jnp.eye(P_SIZE, dtype=jnp.float32)
    offdiag = (noise + jnp.swapaxes(noise, 1, 2)) * (0.5 / math.sqrt(P_SIZE))
    return (offdiag * (1.0 - unit) + unit * diag[:, :, None]).astype(jnp.bfloat16)


def draw_right_diag(key, part):
    key = jax.random.fold_in(key, 3)
    first, second = jax.random.split(key)
    noise = jax.random.normal(first, (SEGS * Q, P_SIZE, P_SIZE), jnp.float32)
    diag = jax.random.uniform(second, (SEGS * Q, P_SIZE), jnp.float32, 1.0, 3.0)
    unit = jnp.eye(P_SIZE, dtype=jnp.float32)
    offdiag = (noise + jnp.swapaxes(noise, 1, 2)) * (0.5 / math.sqrt(P_SIZE))
    return (offdiag * (1.0 - unit) + unit * diag[:, :, None]).astype(jnp.bfloat16)


def touch_ends(drawn, key, low, top_value):
    dims = drawn.shape
    place = [jax.random.randint(jax.random.fold_in(key, axis), (), 0, dims[axis]) for axis in range(len(dims))]
    drawn = drawn.at[tuple(place)].set(low)
    longest = dims.index(max(dims))
    place[longest] = (place[longest] + 1) % dims[longest]
    return drawn.at[tuple(place)].set(top_value)


def block_scale(own_key, shape, cuts, low, high):
    level, own = 1.0, jax.random.fold_in(own_key, 6)
    for dim, parts in cuts:
        draws = jnp.exp(jax.random.uniform(jax.random.fold_in(own, dim), (parts,), jnp.float32, low / len(cuts), high / len(cuts)))
        level = level * jnp.repeat(draws, shape[dim] // parts).reshape([-1 if axis == dim else 1 for axis in range(len(shape))])
    return level


def scatter_about(rng, dims, deviation, limit, cuts=(), kind=jnp.bfloat16):
    gain = block_scale(rng, dims, cuts, -0.22, 0.18) if cuts else 1.0
    drawn = jax.random.normal(rng, dims, jnp.float32) * deviation * gain
    return jnp.minimum(jnp.maximum(drawn, -limit), limit).astype(kind)


def setup_inputs(seed: int = 0) -> dict:
    keys = jax.random.split(jax.random.key(seed), 10)
    start_state = scatter_about(keys[0], (SEGS * Q, P_SIZE, P_SIZE), 1.0, 6.0, ((0, 32),), jnp.float32)
    sector_sizes = draw_sector_sizes(jax.random.fold_in(keys[9], 71), 0)
    partner = touch_ends(jax.random.randint(keys[2], (SEGS * Q, K), 0, Q), jax.random.fold_in(keys[2], 1), 0, Q - 1).astype(jnp.int32)
    left_diag = draw_left_diag(jax.random.fold_in(keys[9], 71), 0)
    right_diag = draw_right_diag(jax.random.fold_in(keys[9], 71), 0)
    left_hop = scatter_about(keys[5], (SEGS * Q, K, P_SIZE, P_SIZE), P_SIZE ** -0.5, 0.375, ((0, 32),))
    right_hop = scatter_about(keys[6], (SEGS * Q, K, P_SIZE, P_SIZE), P_SIZE ** -0.5, 0.375, ((0, 32),))
    left_coupling = jnp.clip(jnp.exp(math.log(3.0) - 2.3025851 * jax.random.uniform(keys[7], (SEGS, K + 1), jnp.float32) ** block_scale(keys[7], (SEGS, K + 1), ((0, 4),), -0.2, 0.2)), 0.3, 3.0)
    right_coupling = jnp.clip(jnp.exp(math.log(3.0) - 2.3025851 * jax.random.uniform(keys[8], (SEGS, K + 1), jnp.float32) ** block_scale(keys[8], (SEGS, K + 1), ((0, 4),), -0.2, 0.2)), 0.3, 3.0)
    return dict(start_state=start_state, sector_sizes=sector_sizes, partner=partner, left_diag=left_diag, right_diag=right_diag, left_hop=left_hop, right_hop=right_hop, left_coupling=left_coupling, right_coupling=right_coupling)


EPS = 1e-06

def rotate(rayleigh, coupling, curvature):
    half = 0.5 * (curvature - rayleigh)
    radius = jnp.sqrt(half * half + coupling * coupling)
    lowest = 0.5 * (rayleigh + curvature) - radius
    return (radius + half, -coupling, lowest)

def segment(items):
    start_state, sizes, partner, left_diag, right_diag, left_hop, right_hop = items
    index = jnp.arange(P_SIZE)
    live = (index[None, :, None] < sizes[:, None, None]) & (index[None, None, :] < sizes[:, None, None])
    mask = live.astype(jnp.float32)
    hdiag = jnp.diagonal(left_diag, axis1=1, axis2=2).astype(jnp.float32)[:, :, None] + jnp.diagonal(right_diag, axis1=1, axis2=2).astype(jnp.float32)[:, None, :]

    def apply(field):
        rounded = field.astype(jnp.bfloat16).astype(jnp.float32)
        own = jnp.einsum('qij,qjk->qik', left_diag.astype(jnp.float32), rounded) + jnp.einsum('qij,qjk->qik', rounded, right_diag.astype(jnp.float32))
        source = rounded[partner]
        middle = jnp.einsum('qkij,qkjl->qkil', left_hop.astype(jnp.float32), source).astype(jnp.bfloat16)
        hop = jnp.einsum('qkij,qkjl->qil', middle.astype(jnp.float32), right_hop.astype(jnp.float32))
        return (own + hop) * mask

    def total(first, second):
        return jnp.sum(first * second)
    state = start_state * mask
    state = state * lax.rsqrt(total(state, state) + EPS)
    image = apply(state)
    lowest = jnp.float32(0.0)
    for step in range(ITERS):
        rayleigh = total(state, image)
        correction = (image - rayleigh * state) / hdiag
        correlation = total(state, correction)
        correction = correction - correlation * state
        spread = total(correction, correction)
        direction = correction * lax.rsqrt(spread + EPS)
        pushed = apply(direction)
        coupling = total(state, pushed)
        curvature = total(direction, pushed)
        alpha, beta, lowest = rotate(rayleigh, coupling, curvature)
        state = alpha * state + beta * direction
        image = alpha * image + beta * pushed
        scale = lax.rsqrt(total(state, state) + EPS)
        state = state * scale
        image = image * scale
    scaled = (state * (P_SIZE * math.sqrt(Q))).astype(jnp.bfloat16).astype(jnp.float32)
    left_ops = jnp.concatenate([left_diag[:, None], left_hop], axis=1).astype(jnp.float32)
    right_ops = jnp.concatenate([right_diag[:, None], right_hop], axis=1).astype(jnp.float32)
    left_mid = jnp.einsum('qcij,qjb->qcib', left_ops, scaled).astype(jnp.bfloat16).astype(jnp.float32)
    left_env = (jnp.einsum('qia,qcib->qcab', scaled, left_mid) / P_SIZE).astype(jnp.bfloat16)
    right_mid = jnp.einsum('qai,qcij->qcaj', scaled, right_ops).astype(jnp.bfloat16).astype(jnp.float32)
    right_env = (jnp.einsum('qcaj,qbj->qcab', right_mid, scaled) / P_SIZE).astype(jnp.bfloat16)
    return (state, lowest, left_env, right_env)

def reference(start_state, sector_sizes, partner, left_diag, right_diag, left_hop, right_hop, left_coupling, right_coupling):
    items = (start_state.reshape(SEGS, Q, P_SIZE, P_SIZE), sector_sizes.reshape(SEGS, Q), partner.reshape(SEGS, Q, K), left_diag.reshape(SEGS, Q, P_SIZE, P_SIZE), right_diag.reshape(SEGS, Q, P_SIZE, P_SIZE), left_hop.reshape(SEGS, Q, K, P_SIZE, P_SIZE), right_hop.reshape(SEGS, Q, K, P_SIZE, P_SIZE))
    state, energy, left_env, right_env = lax.map(segment, items)
    zero_block = jnp.zeros((1, Q, P_SIZE, P_SIZE), jnp.float32)
    left_from = jnp.einsum('sc,sqcab->sqab', left_coupling[1:], left_env[:-1].astype(jnp.float32))
    left_boundary = jnp.concatenate([zero_block, left_from], axis=0).astype(jnp.bfloat16)
    right_from = jnp.einsum('sc,sqcab->sqab', right_coupling[:-1], right_env[1:].astype(jnp.float32))
    right_boundary = jnp.concatenate([right_from, zero_block], axis=0).astype(jnp.bfloat16)
    return (state.reshape(SEGS * Q, P_SIZE, P_SIZE), energy, left_boundary.reshape(SEGS * Q, P_SIZE, P_SIZE), right_boundary.reshape(SEGS * Q, P_SIZE, P_SIZE))
```

```python
import functools
import math

import jax
import jax.numpy as jnp
from jax import lax
from jax.experimental import pallas as pl
from jax.experimental.pallas import tpu as pltpu
from jax.sharding import PartitionSpec as P

ITERS = 4
EPS = 1e-06
F32 = jnp.float32
BF16 = jnp.bfloat16
MESH = pl.DeviceIdType.MESH


def ring_order(count):
    depth = 4 if count % 4 == 0 else 2
    across = count // depth
    order = [z * across for z in range(depth)]
    for z in reversed(range(depth)):
        row = list(range(1, across))
        if (depth - 1 - z) % 2:
            row.reverse()
        order += [z * across + y for y in row]
    return order


def pick(table, index):
    value = jnp.int32(table[0])
    for place in range(1, len(table)):
        value = jnp.where(index == place, jnp.int32(table[place]), value)
    return value


def dot(first, second, contract=((1,), (0,))):
    return lax.dot_general(first, second, (contract, ((), ())), preferred_element_type=F32)


def kernel(
    group,
    segments,
    sizes_ref,
    partner_ref,
    start_ref,
    ldiag_ref,
    rdiag_ref,
    lcoup_ref,
    rcoup_ref,
    lhop_ref,
    rhop_ref,
    state_ref,
    energy_ref,
    lbound_ref,
    rbound_ref,
    left_ops,
    right_ops,
    field,
    middle,
    v_ref,
    h_ref,
    p_ref,
    q_ref,
    inverse_ref,
    sums,
    coup_out,
    coup_in,
    mix_left,
    mix_right,
    edge_out,
    edge_in,
    load_sem,
    ring_send,
    ring_recv,
    sum_send,
    sum_recv,
    coup_send,
    coup_recv,
    edge_send,
    edge_recv,
):
    seg = lax.axis_index("seg")
    me = lax.axis_index("blk")
    width = start_ref.shape[1]
    channels = lhop_ref.shape[1]
    half = width // 2
    has_next = seg < segments - 1
    has_prev = seg > 0

    loads = (
        pltpu.make_async_copy(lhop_ref.at[0], left_ops, load_sem.at[0]),
        pltpu.make_async_copy(rhop_ref.at[0], right_ops, load_sem.at[1]),
    )
    for load in loads:
        load.start()

    barrier = pltpu.get_barrier_semaphore()
    for step in range(1, group):
        pl.semaphore_signal(
            barrier, inc=1, device_id={"blk": lax.rem(me + step, group)}, device_id_type=MESH
        )

    @pl.when(has_next)
    def _():
        pl.semaphore_signal(barrier, inc=1, device_id={"seg": seg + 1}, device_id_type=MESH)

    @pl.when(has_prev)
    def _():
        pl.semaphore_signal(barrier, inc=1, device_id={"seg": seg - 1}, device_id_type=MESH)

    size = sizes_ref[0]
    rows = lax.broadcasted_iota(jnp.int32, (width, width), 0)
    cols = lax.broadcasted_iota(jnp.int32, (width, width), 1)
    on_diag = rows == cols
    left_line = jnp.sum(
        jnp.where(on_diag, ldiag_ref[0].astype(F32), 0.0), axis=1, keepdims=True
    )
    right_line = jnp.sum(
        jnp.where(on_diag, rdiag_ref[0].astype(F32), 0.0), axis=0, keepdims=True
    )
    inverse_ref[...] = 1.0 / (left_line + right_line)

    def masked(value):
        return jnp.where((rows < size) & (cols < size), value, 0.0)

    p_ref[...] = masked(start_ref[0])
    field[me] = p_ref[...].astype(BF16)
    coup_out[...] = jnp.zeros_like(coup_out)
    coup_out[0, 0:1, 0 : channels + 1] = lcoup_ref[...]
    coup_out[1, 0:1, 0 : channels + 1] = rcoup_ref[...]

    others = jnp.int32(group - 1) + has_next.astype(jnp.int32) + has_prev.astype(jnp.int32)
    pl.semaphore_wait(barrier, others)

    order = ring_order(group)
    place = [order.index(blk) for blk in range(group)]

    def along(step):
        return pick([order[(place[blk] + step) % group] for blk in range(group)], me)

    far = group // 2
    source = [[along(-1 - j) for j in range(far)], [along(1 + j) for j in range(far)]]
    target = [source[1][0], source[0][0]]
    lanes = [(0, 0), (1, 1), (0, 1), (1, 0)]

    def count(side, part):
        return far if side == part else far - 1

    def ring(side, part, j, slot):
        piece = field.at[slot, pl.ds(part * half, half), :]
        return pltpu.make_async_remote_copy(
            src_ref=piece,
            dst_ref=piece,
            send_sem=ring_send.at[side, part, j],
            recv_sem=ring_recv.at[side, part, j],
            device_id={"blk": target[side]},
            device_id_type=MESH,
        )

    def send_own():
        for side, part in lanes:
            ring(side, part, 0, me).start()

    def pass_on():
        for j in range(far):
            for side, part in lanes:
                if j < count(side, part):
                    ring(side, part, j, source[side][j]).wait_recv()
                    if j + 1 < count(side, part):
                        ring(side, part, j + 1, source[side][j]).start()

    def drain():
        for side, part in lanes:
            for j in range(count(side, part)):
                slot = me if j == 0 else source[side][j - 1]
                ring(side, part, j, slot).wait_send()

    def sum_copy(step):
        return pltpu.make_async_remote_copy(
            src_ref=sums.at[me],
            dst_ref=sums.at[me],
            send_sem=sum_send.at[step],
            recv_sem=sum_recv.at[step],
            device_id={"blk": lax.rem(me + step, group)},
            device_id_type=MESH,
        )

    def totals(products):
        for place_, (first, second) in enumerate(products):
            line = jnp.sum(first * second, axis=0, keepdims=True)
            short = line[:, 0:128]
            for begin in range(128, width, 128):
                short = short + line[:, begin : begin + 128]
            sums[me, place_ : place_ + 1, :] = short
        for step in range(1, group):
            sum_copy(step).start()
        for step in range(1, group):
            sum_copy(step).wait()
        whole = sums[0]
        for blk in range(1, group):
            whole = whole + sums[blk]
        whole = jnp.sum(whole, axis=1, keepdims=True)
        return [whole[i : i + 1, :] for i in range(len(products))]

    def own_terms():
        own = field[me]
        q_ref[...] = dot(ldiag_ref[0], own) + dot(own, rdiag_ref[0])

    def hop_terms():
        for k in range(channels):
            block = field[partner_ref[0, k]]
            middle[:, k * width : (k + 1) * width] = dot(left_ops[k], block).astype(BF16)
        q_ref[...] = masked(
            q_ref[...] + dot(middle[...], right_ops[...].reshape(channels * width, width))
        )

    def next_correction(rayleigh):
        p_ref[...] = (h_ref[...] - rayleigh * v_ref[...]) * inverse_ref[...]
        field[me] = p_ref[...].astype(BF16)

    def coup_copy(which):
        shift = -1 if which == 0 else 1
        return pltpu.make_async_remote_copy(
            src_ref=coup_out.at[which],
            dst_ref=coup_in.at[which],
            send_sem=coup_send.at[which],
            recv_sem=coup_recv.at[which],
            device_id={"seg": seg + shift},
            device_id_type=MESH,
        )

    def mix(which, diag_ref, ops, mixed):
        weights = coup_in[which]
        mixed_sum = weights[0:1, 0:1] * diag_ref[0].astype(F32)
        for k in range(channels):
            mixed_sum = mixed_sum + weights[0:1, k + 1 : k + 2] * ops[k].astype(F32)
        mixed[...] = mixed_sum.astype(BF16)

    send_own()

    @pl.when(has_prev)
    def _():
        coup_copy(0).start()

    @pl.when(has_next)
    def _():
        coup_copy(1).start()

    own_terms()
    for load in loads:
        load.wait()

    @pl.when(has_next)
    def _():
        coup_copy(0).wait_recv()
        mix(0, ldiag_ref, left_ops, mix_left)

    @pl.when(has_prev)
    def _():
        coup_copy(1).wait_recv()
        mix(1, rdiag_ref, right_ops, mix_right)

    pass_on()
    hop_terms()
    drain()
    p = p_ref[...]
    pp, pq = totals([(p, p), (p, q_ref[...])])
    scale = lax.rsqrt(pp + EPS)
    v_ref[...] = scale * p
    h_ref[...] = scale * q_ref[...]
    next_correction(scale * scale * pq)

    def iterate(_, lowest):
        send_own()
        own_terms()
        pass_on()
        hop_terms()
        drain()
        v, h, p, q = v_ref[...], h_ref[...], p_ref[...], q_ref[...]
        vv, vp, pp, vh, vq, ph, pq = totals(
            [(v, v), (v, p), (p, p), (v, h), (v, q), (p, h), (p, q)]
        )
        g = vp
        spread = jnp.maximum(pp - 2.0 * g * vp + g * g * vv, 0.0)
        unit = lax.rsqrt(spread + EPS)
        coupling = unit * (vq - g * vh)
        curvature = unit * unit * (pq - g * ph - g * vq + g * g * vh)
        bend = 0.5 * (curvature - vh)
        radius = jnp.sqrt(bend * bend + coupling * coupling)
        lowest = 0.5 * (vh + curvature) - radius
        alpha, beta = radius + bend, -coupling
        vu = unit * (vp - g * vv)
        uu = unit * unit * spread
        newsq = alpha * alpha * vv + 2.0 * alpha * beta * vu + beta * beta * uu
        scale = lax.rsqrt(newsq + EPS)
        with_p = scale * beta * unit
        with_v = scale * alpha - with_p * g
        v_ref[...] = with_v * v + with_p * p
        h_ref[...] = with_v * h + with_p * q
        rayleigh = with_v * with_v * vh + with_v * with_p * (vq + ph) + with_p * with_p * pq
        next_correction(rayleigh)
        return lowest

    lowest = lax.fori_loop(0, ITERS, iterate, jnp.zeros((1, 1), F32))
    energy_ref[...] = lowest
    state_ref[0] = v_ref[...]
    z = (v_ref[...] * (width * math.sqrt(group))).astype(BF16)

    def edge_copy(which):
        shift = 1 if which == 0 else -1
        return pltpu.make_async_remote_copy(
            src_ref=edge_out.at[which],
            dst_ref=edge_in.at[which],
            send_sem=edge_send.at[which],
            recv_sem=edge_recv.at[which],
            device_id={"seg": seg + shift},
            device_id_type=MESH,
        )

    @pl.when(has_next)
    def _():
        inner = dot(mix_left[...], z).astype(BF16)
        edge_out[0] = (dot(z, inner, ((0,), (0,))) * (1.0 / width)).astype(BF16)
        edge_copy(0).start()

    @pl.when(has_prev)
    def _():
        inner = dot(z, mix_right[...]).astype(BF16)
        edge_out[1] = (dot(inner, z, ((1,), (1,))) * (1.0 / width)).astype(BF16)
        edge_copy(1).start()

    @pl.when(has_prev)
    def _():
        coup_copy(0).wait_send()
        edge_copy(0).wait_recv()
        lbound_ref[0] = edge_in[0]
        edge_copy(1).wait_send()

    @pl.when(jnp.logical_not(has_prev))
    def _():
        lbound_ref[...] = jnp.zeros_like(lbound_ref)

    @pl.when(has_next)
    def _():
        coup_copy(1).wait_send()
        edge_copy(1).wait_recv()
        rbound_ref[0] = edge_in[1]
        edge_copy(0).wait_send()

    @pl.when(jnp.logical_not(has_next))
    def _():
        rbound_ref[...] = jnp.zeros_like(rbound_ref)


def on_device(
    group,
    segments,
    start_state,
    sector_sizes,
    partner,
    left_diag,
    right_diag,
    left_hop,
    right_hop,
    left_coupling,
    right_coupling,
):
    width = start_state.shape[1]
    channels = left_hop.shape[1]
    far = group // 2
    vmem = pl.BlockSpec(memory_space=pltpu.VMEM)
    smem = pl.BlockSpec(memory_space=pltpu.SMEM)
    hbm = pl.BlockSpec(memory_space=pl.ANY)
    square = (width, width)
    state, energy, left_boundary, right_boundary = pl.pallas_call(
        functools.partial(kernel, group, segments),
        out_shape=(
            jax.ShapeDtypeStruct((1,) + square, F32),
            jax.ShapeDtypeStruct((1, 1), F32),
            jax.ShapeDtypeStruct((1,) + square, BF16),
            jax.ShapeDtypeStruct((1,) + square, BF16),
        ),
        in_specs=[smem, smem, vmem, vmem, vmem, vmem, vmem, hbm, hbm],
        out_specs=(vmem, vmem, vmem, vmem),
        scratch_shapes=[
            pltpu.VMEM((channels,) + square, BF16),
            pltpu.VMEM((channels,) + square, BF16),
            pltpu.VMEM((group,) + square, BF16),
            pltpu.VMEM((width, channels * width), BF16),
            pltpu.VMEM(square, F32),
            pltpu.VMEM(square, F32),
            pltpu.VMEM(square, F32),
            pltpu.VMEM(square, F32),
            pltpu.VMEM(square, F32),
            pltpu.VMEM((group, 8, 128), F32),
            pltpu.VMEM((2, 8, 128), F32),
            pltpu.VMEM((2, 8, 128), F32),
            pltpu.VMEM(square, BF16),
            pltpu.VMEM(square, BF16),
            pltpu.VMEM((2,) + square, BF16),
            pltpu.VMEM((2,) + square, BF16),
            pltpu.SemaphoreType.DMA((2,)),
            pltpu.SemaphoreType.DMA((2, 2, far)),
            pltpu.SemaphoreType.DMA((2, 2, far)),
            pltpu.SemaphoreType.DMA((group,)),
            pltpu.SemaphoreType.DMA((group,)),
            pltpu.SemaphoreType.DMA((2,)),
            pltpu.SemaphoreType.DMA((2,)),
            pltpu.SemaphoreType.DMA((2,)),
            pltpu.SemaphoreType.DMA((2,)),
        ],
        compiler_params=pltpu.CompilerParams(
            collective_id=0, has_side_effects=True, vmem_limit_bytes=40 * 1024 * 1024
        ),
    )(
        sector_sizes,
        partner,
        start_state,
        left_diag,
        right_diag,
        left_coupling,
        right_coupling,
        left_hop,
        right_hop,
    )
    return state, jnp.reshape(energy, (1,)), left_boundary, right_boundary


def solution(mesh):
    block = P(("seg", "blk"), None, None)
    placed = (
        block,
        P(("seg", "blk")),
        P(("seg", "blk"), None),
        block,
        block,
        P(("seg", "blk"), None, None, None),
        P(("seg", "blk"), None, None, None),
        P("seg", None),
        P("seg", None),
    )
    return jax.shard_map(
        functools.partial(on_device, mesh.shape["blk"], mesh.shape["seg"]),
        mesh=mesh,
        in_specs=placed,
        out_specs=(block, P("seg"), block, block),
        check_vma=False,
    )
```

```python
import functools
import math

import jax
import jax.numpy as jnp
from jax import lax
from jax.experimental import pallas as pl
from jax.experimental.pallas import tpu as pltpu
from jax.sharding import PartitionSpec as P

ITERS = 4
EPS = 1e-06
PARTS = 4
F32 = jnp.float32
BF16 = jnp.bfloat16
MESH = pl.DeviceIdType.MESH


def ring_order(count):
    depth = 4 if count % 4 == 0 else 2
    across = count // depth
    order = [z * across for z in range(depth)]
    for z in reversed(range(depth)):
        row = list(range(1, across))
        if (depth - 1 - z) % 2:
            row.reverse()
        order += [z * across + y for y in row]
    return order


def pick(table, index):
    value = jnp.int32(table[0])
    for place in range(1, len(table)):
        value = jnp.where(index == place, jnp.int32(table[place]), value)
    return value


def dot(first, second, contract=((1,), (0,))):
    return lax.dot_general(first, second, (contract, ((), ())), preferred_element_type=F32)


def kernel(
    group,
    segments,
    sizes_in,
    partner_in,
    start_in,
    ldiag_in,
    rdiag_in,
    lcoup_in,
    rcoup_in,
    lhop_in,
    rhop_in,
    state_ref,
    energy_ref,
    lbound_ref,
    rbound_ref,
    sizes_ref,
    partner_ref,
    start_ref,
    ldiag_ref,
    rdiag_ref,
    lcoup_ref,
    rcoup_ref,
    left_ops,
    right_ops,
    field,
    middle,
    v_ref,
    h_ref,
    p_ref,
    q_ref,
    inverse_ref,
    sums,
    coup_out,
    coup_in,
    mix_left,
    mix_right,
    edge_out,
    edge_in,
    load_sem,
    ring_send,
    ring_recv,
    sum_send,
    sum_recv,
    coup_send,
    coup_recv,
    edge_send,
    edge_recv,
):
    seg = lax.axis_index("seg")
    me = lax.axis_index("blk")
    width = start_ref.shape[1]
    channels = lhop_in.shape[1]
    half = width // PARTS
    has_next = seg < segments - 1
    has_prev = seg > 0

    pairs = (
        (start_in, start_ref),
        (sizes_in, sizes_ref),
        (partner_in, partner_ref),
        (ldiag_in, ldiag_ref),
        (rdiag_in, rdiag_ref),
        (lcoup_in, lcoup_ref),
        (rcoup_in, rcoup_ref),
        (lhop_in.at[0], left_ops),
        (rhop_in.at[0], right_ops),
    )
    loads = [
        pltpu.make_async_copy(origin, held, load_sem.at[i])
        for i, (origin, held) in enumerate(pairs)
    ]
    for load in loads:
        load.start()

    barrier = pltpu.get_barrier_semaphore()
    for step in range(1, group):
        pl.semaphore_signal(
            barrier, inc=1, device_id={"blk": lax.rem(me + step, group)}, device_id_type=MESH
        )

    @pl.when(has_next)
    def _():
        pl.semaphore_signal(barrier, inc=1, device_id={"seg": seg + 1}, device_id_type=MESH)

    @pl.when(has_prev)
    def _():
        pl.semaphore_signal(barrier, inc=1, device_id={"seg": seg - 1}, device_id_type=MESH)

    for load in loads[:7]:
        load.wait()
    size = sizes_ref[0]
    rows = lax.broadcasted_iota(jnp.int32, (width, width), 0)
    cols = lax.broadcasted_iota(jnp.int32, (width, width), 1)
    on_diag = rows == cols
    left_line = jnp.sum(
        jnp.where(on_diag, ldiag_ref[0].astype(F32), 0.0), axis=1, keepdims=True
    )
    right_line = jnp.sum(
        jnp.where(on_diag, rdiag_ref[0].astype(F32), 0.0), axis=0, keepdims=True
    )
    inverse_ref[...] = 1.0 / (left_line + right_line)

    def masked(value):
        return jnp.where((rows < size) & (cols < size), value, 0.0)

    p_ref[...] = masked(start_ref[0])
    field[me] = p_ref[...].astype(BF16)
    coup_out[...] = jnp.zeros_like(coup_out)
    coup_out[0, 0:1, 0 : channels + 1] = lcoup_ref[...]
    coup_out[1, 0:1, 0 : channels + 1] = rcoup_ref[...]

    others = jnp.int32(group - 1) + has_next.astype(jnp.int32) + has_prev.astype(jnp.int32)
    pl.semaphore_wait(barrier, others)

    order = ring_order(group)
    place = [order.index(blk) for blk in range(group)]

    def along(step):
        return pick([order[(place[blk] + step) % group] for blk in range(group)], me)

    far = group // 2
    source = [[along(-1 - j) for j in range(far)], [along(1 + j) for j in range(far)]]
    target = [source[1][0], source[0][0]]
    first = [lane for i in range(PARTS // 2) for lane in ((0, i), (1, PARTS // 2 + i))]
    lanes = first + [(1 - side, part) for side, part in first]

    def count(side, part):
        return far if side == part // (PARTS // 2) else far - 1

    def ring(side, part, j, slot):
        piece = field.at[slot, pl.ds(part * half, half), :]
        return pltpu.make_async_remote_copy(
            src_ref=piece,
            dst_ref=piece,
            send_sem=ring_send.at[side, part, j],
            recv_sem=ring_recv.at[side, part, j],
            device_id={"blk": target[side]},
            device_id_type=MESH,
        )

    def send_own():
        for side, part in lanes:
            ring(side, part, 0, me).start()

    def pass_on():
        for j in range(far):
            for side, part in lanes:
                if j < count(side, part):
                    ring(side, part, j, source[side][j]).wait_recv()
                    if j + 1 < count(side, part):
                        ring(side, part, j + 1, source[side][j]).start()

    def drain():
        for side, part in lanes:
            for j in range(count(side, part)):
                slot = me if j == 0 else source[side][j - 1]
                ring(side, part, j, slot).wait_send()

    def sum_copy(step):
        return pltpu.make_async_remote_copy(
            src_ref=sums.at[me],
            dst_ref=sums.at[me],
            send_sem=sum_send.at[step],
            recv_sem=sum_recv.at[step],
            device_id={"blk": lax.rem(me + step, group)},
            device_id_type=MESH,
        )

    def totals(products):
        lane = lax.broadcasted_iota(jnp.int32, (1, 128), 1)
        row = jnp.zeros((1, 128), F32)
        for place_, (first, second) in enumerate(products):
            line = jnp.sum(first * second, axis=0, keepdims=True)
            short = line[:, 0:128]
            for begin in range(128, width, 128):
                short = short + line[:, begin : begin + 128]
            row = row + jnp.where(lane == place_, jnp.sum(short, axis=1, keepdims=True), 0.0)
        sums[me] = row
        for step in range(1, group):
            sum_copy(step).start()
        for step in range(1, group):
            sum_copy(step).wait()
        whole = sums[0]
        for blk in range(1, group):
            whole = whole + sums[blk]
        return [whole[:, i : i + 1] for i in range(len(products))]

    def own_terms():
        own = field[me]
        q_ref[...] = dot(ldiag_ref[0], own) + dot(own, rdiag_ref[0])

    def hop_terms():
        for k in range(channels):
            block = field[partner_ref[0, k]]
            middle[:, k * width : (k + 1) * width] = dot(left_ops[k], block).astype(BF16)
        q_ref[...] = masked(
            q_ref[...] + dot(middle[...], right_ops[...].reshape(channels * width, width))
        )

    def next_correction(rayleigh):
        p_ref[...] = (h_ref[...] - rayleigh * v_ref[...]) * inverse_ref[...]
        field[me] = p_ref[...].astype(BF16)

    def coup_copy(which):
        shift = -1 if which == 0 else 1
        return pltpu.make_async_remote_copy(
            src_ref=coup_out.at[which],
            dst_ref=coup_in.at[which],
            send_sem=coup_send.at[which],
            recv_sem=coup_recv.at[which],
            device_id={"seg": seg + shift},
            device_id_type=MESH,
        )

    def mix(which, diag_ref, ops, mixed):
        weights = coup_in[which]
        mixed_sum = weights[0:1, 0:1] * diag_ref[0].astype(F32)
        for k in range(channels):
            mixed_sum = mixed_sum + weights[0:1, k + 1 : k + 2] * ops[k].astype(F32)
        mixed[...] = mixed_sum.astype(BF16)

    send_own()

    @pl.when(has_prev)
    def _():
        coup_copy(0).start()

    @pl.when(has_next)
    def _():
        coup_copy(1).start()

    own_terms()
    for load in loads[7:]:
        load.wait()

    @pl.when(has_next)
    def _():
        coup_copy(0).wait_recv()
        mix(0, ldiag_ref, left_ops, mix_left)

    @pl.when(has_prev)
    def _():
        coup_copy(1).wait_recv()
        mix(1, rdiag_ref, right_ops, mix_right)

    pass_on()
    hop_terms()
    drain()
    p = p_ref[...]
    pp, pq = totals([(p, p), (p, q_ref[...])])
    scale = lax.rsqrt(pp + EPS)
    v_ref[...] = scale * p
    h_ref[...] = scale * q_ref[...]
    next_correction(scale * scale * pq)

    def iterate(_, lowest):
        send_own()
        own_terms()
        pass_on()
        hop_terms()
        drain()
        v, h, p, q = v_ref[...], h_ref[...], p_ref[...], q_ref[...]
        vv, vp, pp, vh, vq, ph, pq = totals(
            [(v, v), (v, p), (p, p), (v, h), (v, q), (p, h), (p, q)]
        )
        g = vp
        spread = jnp.maximum(pp - 2.0 * g * vp + g * g * vv, 0.0)
        unit = lax.rsqrt(spread + EPS)
        coupling = unit * (vq - g * vh)
        curvature = unit * unit * (pq - g * ph - g * vq + g * g * vh)
        bend = 0.5 * (curvature - vh)
        radius = jnp.sqrt(bend * bend + coupling * coupling)
        lowest = 0.5 * (vh + curvature) - radius
        alpha, beta = radius + bend, -coupling
        vu = unit * (vp - g * vv)
        uu = unit * unit * spread
        newsq = alpha * alpha * vv + 2.0 * alpha * beta * vu + beta * beta * uu
        scale = lax.rsqrt(newsq + EPS)
        with_p = scale * beta * unit
        with_v = scale * alpha - with_p * g
        v_ref[...] = with_v * v + with_p * p
        h_ref[...] = with_v * h + with_p * q
        rayleigh = with_v * with_v * vh + with_v * with_p * (vq + ph) + with_p * with_p * pq
        next_correction(rayleigh)
        return lowest

    lowest = lax.fori_loop(0, ITERS, iterate, jnp.zeros((1, 1), F32))
    energy_ref[...] = lowest
    state_ref[0] = v_ref[...]
    z = (v_ref[...] * (width * math.sqrt(group))).astype(BF16)

    def edge_copy(which):
        shift = 1 if which == 0 else -1
        return pltpu.make_async_remote_copy(
            src_ref=edge_out.at[which],
            dst_ref=edge_in.at[which],
            send_sem=edge_send.at[which],
            recv_sem=edge_recv.at[which],
            device_id={"seg": seg + shift},
            device_id_type=MESH,
        )

    @pl.when(has_next)
    def _():
        inner = dot(mix_left[...], z).astype(BF16)
        edge_out[0] = (dot(z, inner, ((0,), (0,))) * (1.0 / width)).astype(BF16)
        edge_copy(0).start()

    @pl.when(has_prev)
    def _():
        inner = dot(z, mix_right[...]).astype(BF16)
        edge_out[1] = (dot(inner, z, ((1,), (1,))) * (1.0 / width)).astype(BF16)
        edge_copy(1).start()

    @pl.when(has_prev)
    def _():
        coup_copy(0).wait_send()
        edge_copy(0).wait_recv()
        lbound_ref[0] = edge_in[0]
        edge_copy(1).wait_send()

    @pl.when(jnp.logical_not(has_prev))
    def _():
        lbound_ref[...] = jnp.zeros_like(lbound_ref)

    @pl.when(has_next)
    def _():
        coup_copy(1).wait_send()
        edge_copy(1).wait_recv()
        rbound_ref[0] = edge_in[1]
        edge_copy(0).wait_send()

    @pl.when(jnp.logical_not(has_next))
    def _():
        rbound_ref[...] = jnp.zeros_like(rbound_ref)


def on_device(
    group,
    segments,
    start_state,
    sector_sizes,
    partner,
    left_diag,
    right_diag,
    left_hop,
    right_hop,
    left_coupling,
    right_coupling,
):
    width = start_state.shape[1]
    channels = left_hop.shape[1]
    far = group // 2
    vmem = pl.BlockSpec(memory_space=pltpu.VMEM)
    hbm = pl.BlockSpec(memory_space=pl.ANY)
    square = (width, width)
    state, energy, left_boundary, right_boundary = pl.pallas_call(
        functools.partial(kernel, group, segments),
        out_shape=(
            jax.ShapeDtypeStruct((1,) + square, F32),
            jax.ShapeDtypeStruct((1, 1), F32),
            jax.ShapeDtypeStruct((1,) + square, BF16),
            jax.ShapeDtypeStruct((1,) + square, BF16),
        ),
        in_specs=[hbm] * 9,
        out_specs=(vmem, vmem, vmem, vmem),
        scratch_shapes=[
            pltpu.SMEM(sector_sizes.shape, jnp.int32),
            pltpu.SMEM(partner.shape, jnp.int32),
            pltpu.VMEM((1,) + square, F32),
            pltpu.VMEM((1,) + square, BF16),
            pltpu.VMEM((1,) + square, BF16),
            pltpu.VMEM(left_coupling.shape, F32),
            pltpu.VMEM(right_coupling.shape, F32),
            pltpu.VMEM((channels,) + square, BF16),
            pltpu.VMEM((channels,) + square, BF16),
            pltpu.VMEM((group,) + square, BF16),
            pltpu.VMEM((width, channels * width), BF16),
            pltpu.VMEM(square, F32),
            pltpu.VMEM(square, F32),
            pltpu.VMEM(square, F32),
            pltpu.VMEM(square, F32),
            pltpu.VMEM(square, F32),
            pltpu.VMEM((group, 1, 128), F32),
            pltpu.VMEM((2, 8, 128), F32),
            pltpu.VMEM((2, 8, 128), F32),
            pltpu.VMEM(square, BF16),
            pltpu.VMEM(square, BF16),
            pltpu.VMEM((2,) + square, BF16),
            pltpu.VMEM((2,) + square, BF16),
            pltpu.SemaphoreType.DMA((9,)),
            pltpu.SemaphoreType.DMA((2, PARTS, far)),
            pltpu.SemaphoreType.DMA((2, PARTS, far)),
            pltpu.SemaphoreType.DMA((group,)),
            pltpu.SemaphoreType.DMA((group,)),
            pltpu.SemaphoreType.DMA((2,)),
            pltpu.SemaphoreType.DMA((2,)),
            pltpu.SemaphoreType.DMA((2,)),
            pltpu.SemaphoreType.DMA((2,)),
        ],
        compiler_params=pltpu.CompilerParams(
            collective_id=0, has_side_effects=True, vmem_limit_bytes=60 * 1024 * 1024
        ),
    )(
        sector_sizes,
        partner,
        start_state,
        left_diag,
        right_diag,
        left_coupling,
        right_coupling,
        left_hop,
        right_hop,
    )
    return state, jnp.reshape(energy, (1,)), left_boundary, right_boundary


def solution(mesh):
    block = P(("seg", "blk"), None, None)
    placed = (
        block,
        P(("seg", "blk")),
        P(("seg", "blk"), None),
        block,
        block,
        P(("seg", "blk"), None, None, None),
        P(("seg", "blk"), None, None, None),
        P("seg", None),
        P("seg", None),
    )
    return jax.shard_map(
        functools.partial(on_device, mesh.shape["blk"], mesh.shape["seg"]),
        mesh=mesh,
        in_specs=placed,
        out_specs=(block, P("seg"), block, block),
        check_vma=False,
    )
```
